128 devices in a mesh: branch: 8 (over y, core), mp: 16 (over z, x).
Axes of the slice: x: 4, y: 4, z: 4, core: 2. Of those that a mesh axis runs over, the one named last changes fastest.
Arguments:
- tokens: bfloat16 [768, 8192], P('mp'), may hold values from -6 to 6
- cotangent: bfloat16 [768, 8192], P('mp'), may hold values from -6 to 6
- routes: int32 [768, 2], P('mp'), may hold values from 0 to 3, all different within a row; in each aligned block of 48 rows (0 to 47, 48 to 95, ...) at most 30 rows name the same one
- router_gates: float32 [768, 2], P('mp'), may hold values from 0.1 to 0.9
- expert_in: bfloat16 [2, 8192, 57344], P(None, None, ('branch', 'mp')), may hold values from -0.0625 to 0.0625
- expert_down: bfloat16 [57344, 8192], P('branch', 'mp'), may hold values from -0.046875 to 0.046875
Outputs:
- layer_output: bfloat16 [768, 8192], P('mp', 'branch')
- token_grads: bfloat16 [768, 8192], P('mp', 'branch')
The draws below stay inside these ranges and needn't reach their ends.
Inputs may be any that keep to these rules, and one draw needn't show every extreme that they name: `routes`: each row names 2 different experts. Among the tokens of one index of mp no expert is named more than 30 times, and in every draw some expert is named exactly 30 times there.
All inputs are finite; a program needn't handle non-finite values.
Results may differ from the reference program's by a relative error of at most 0.023.
Values may be sent and summed in bfloat16 or wider, within the bound.
A program may use at most 192 MiB of HBM per device.

```python
import math
import jax
import jax.numpy as jnp
import numpy as np
from jax import lax

D = 8192
FF = 14336
EXPERTS = 4
TOP = 2
TOK_M = 48
CAP = 30
TOKENS = 768
FF_BLK = 448
N_BRANCH = 8
N_MP = 16


def level_of(key, shape, shards, low, largest):
    def one(axis_at, shards_of):
        draws = jax.random.uniform(jax.random.fold_in(jax.random.fold_in(key, 6), axis_at), (shards_of,), jnp.float32, low / len(shards), largest / len(shards))
        return jnp.repeat(jnp.exp(draws), shape[axis_at] // shards_of).reshape((-1,) + (1,) * (len(shape) - axis_at - 1))

    factor_of = one(*shards[0])
    for cut in shards[1:]:
        factor_of = factor_of * one(*cut)
    return factor_of


def routed_block(rng, own, number, rows, amount, top, limit, skew):
    sequence = jax.random.permutation(rng, amount)
    crowded, ordinary = load_shares(amount, rows * top, limit, skew, True), load_shares(amount, rows * top, limit, skew, False)
    places = jnp.arange(amount)

    def named(tallies, offset_by):
        used = int((tallies > 0).sum())
        fixed = max(1, used // 4)
        shifted = fixed + (places - fixed + offset_by * (used - fixed)) % max(1, amount - fixed)
        return jnp.zeros((amount,), jnp.int32).at[sequence[jnp.where(places < fixed, places, shifted)]].set(jnp.asarray(tallies, jnp.int32))

    tallies = jnp.where(number % 4 == 0, named(crowded, number // 4), named(ordinary, number - number // 4 - 1))
    mixed = jax.random.permutation(jax.random.fold_in(own, 3), amount)
    donor, receiver = mixed[0:amount // 2 * 2:2], mixed[1:amount // 2 * 2:2]
    room = jnp.minimum(tallies[donor] - 1, limit - tallies[receiver]) // 2
    room = jnp.where((donor == sequence[0]) | (receiver == sequence[0]) | (tallies[receiver] == 0), 0, jnp.maximum(room, 0))
    shifted = jax.random.randint(jax.random.fold_in(own, 4), (amount // 2,), 0, 1 << 20) % (room + 1)
    tallies = tallies.at[donor].add(-shifted).at[receiver].add(shifted)
    items = jnp.searchsorted(jnp.cumsum(tallies), jnp.arange(rows * top), side="right").astype(jnp.int32)
    table = items.reshape(top, rows).T
    table = table[jax.random.permutation(jax.random.fold_in(own, 1), rows)]
    offset_by = jax.random.randint(jax.random.fold_in(own, 2), (rows, 1), 0, top)
    return jnp.take_along_axis(table, (jnp.arange(top)[None, :] + offset_by) % top, axis=1)


def load_shares(count, total, bound, slope, full):
    weights = [(1 << 20) // math.isqrt(standing ** slope) + 1 for standing in range(1, count + 1)]
    largest = bound if full else min(bound, max(-(-total // count), total * weights[0] // sum(weights)))
    least = 1 if total - largest >= count - 1 else 0
    counts, spare = [largest] + [least] * (count - 1), total - largest - least * (count - 1)
    while spare > 0:
        movable = [i for i in range(1, count) if counts[i] < largest] or [i for i in range(1, count) if counts[i] < bound]
        pool, remaining = sum([weights[i] for i in movable]), spare
        for i in movable:
            more = min(bound - counts[i], max(1, remaining * weights[i] // pool), spare)
            counts[i] = counts[i] + more
            spare = spare - more
    return np.array(counts)


def gaussian(own_key, extent, width, bound, shards=(), kind=jnp.bfloat16):
    array = jax.random.normal(own_key, extent, jnp.float32) * width
    if len(shards) > 0:
        array = level_of(own_key, extent, shards, -0.22, 0.18) * array
    return jnp.clip(array, min=-bound, max=bound).astype(kind)


def setup_inputs(seed: int = 0) -> dict:
    splits = jax.random.split(jax.random.key(seed), 7)
    tokens = gaussian(splits[0], (TOKENS, D), 1.0, 6.0, ((0, 16),))
    cotangent = gaussian(splits[1], (TOKENS, D), 1.0, 6.0, ((0, 16),))
    routes_keys = jax.random.split(jax.random.fold_in(splits[2], 1), TOKENS // TOK_M)
    routes_turns = jax.random.permutation(jax.random.fold_in(splits[2], 3), TOKENS // TOK_M)
    routes = jax.vmap(lambda own, number: routed_block(jax.random.fold_in(splits[2], 2), own, number, TOK_M, EXPERTS, TOP, CAP, 2))(routes_keys, routes_turns).reshape((TOKENS, TOP))
    router_gates = jnp.clip(0.1 + 0.79999997 * jax.random.uniform(splits[3], (TOKENS, TOP), jnp.float32) ** level_of(splits[3], (TOKENS, TOP), ((0, 16),), -0.2, 0.2), 0.1, 0.9)
    expert_in = gaussian(splits[4], (2, D, EXPERTS * FF), D ** -0.5, 0.0625, ((2, 128),))
    expert_down = gaussian(splits[5], (EXPERTS * FF, D), FF ** -0.5, 0.046875, ((0, 8), (1, 16)))
    return {"tokens": tokens, "cotangent": cotangent, "routes": routes, "router_gates": router_gates, "expert_in": expert_in, "expert_down": expert_down}


def round_trip(value):
    return lax.optimization_barrier(value.astype(jnp.bfloat16)).astype(jnp.float32)


def contract_last(left, right):
    return lax.dot_general(left, right, (((1,), (1,)), ((), ())), preferred_element_type=jnp.float32)


def slot_table(block_routes, expert):
    chosen = jnp.any(block_routes == expert, axis=-1)
    counted = chosen.astype(jnp.int32)
    places = jnp.cumsum(counted, axis=-1) - counted
    return chosen, places


def reference(tokens, cotangent, routes, router_gates, expert_in, expert_down):
    slot_count = N_MP * CAP
    blocks = routes.reshape(N_MP, TOK_M, TOP)
    outputs = jnp.zeros((TOKENS, D), jnp.float32)
    grads = jnp.zeros((TOKENS, D), jnp.float32)
    block_count = N_BRANCH * N_MP // EXPERTS
    for expert in range(EXPERTS):
        chosen, places = slot_table(blocks, expert)
        offsets = jnp.arange(N_MP, dtype=jnp.int32)[:, None] * CAP
        target = jnp.where(chosen, offsets + places, slot_count).reshape(-1).astype(jnp.int32)
        inputs = jnp.zeros((slot_count, D), jnp.bfloat16).at[target].set(tokens, mode="drop")
        grad_rows = jnp.zeros((slot_count, D), jnp.bfloat16).at[target].set(cotangent, mode="drop")
        gate_all = expert_in[0][:, expert * FF:(expert + 1) * FF]
        up_all = expert_in[1][:, expert * FF:(expert + 1) * FF]
        down_all = expert_down[expert * FF:(expert + 1) * FF]

        def block_step(totals, block_id):
            block_start = (block_id * FF_BLK).astype(jnp.int32)
            gate_blk = lax.dynamic_slice_in_dim(gate_all, block_start, FF_BLK, 1)
            up_blk = lax.dynamic_slice_in_dim(up_all, block_start, FF_BLK, 1)
            down_blk = lax.dynamic_slice_in_dim(down_all, block_start, FF_BLK, 0)
            pre_gate = jnp.dot(inputs, gate_blk, preferred_element_type=jnp.float32)
            pre_up = jnp.dot(inputs, up_blk, preferred_element_type=jnp.float32)
            sigmoid_gate = jax.nn.sigmoid(pre_gate)
            active = (pre_gate * sigmoid_gate * pre_up).astype(jnp.bfloat16)
            part_out = round_trip(jnp.dot(active, down_blk, preferred_element_type=jnp.float32))
            back_hidden = contract_last(grad_rows, down_blk)
            gate_grad = (back_hidden * pre_up * sigmoid_gate * (1.0 + pre_gate * (1.0 - sigmoid_gate))).astype(jnp.bfloat16)
            up_grad = (back_hidden * pre_gate * sigmoid_gate).astype(jnp.bfloat16)
            part_in = round_trip(contract_last(gate_grad, gate_blk) + contract_last(up_grad, up_blk))
            return (totals[0] + part_out, totals[1] + part_in), None

        start_totals = (jnp.zeros((slot_count, D), jnp.float32), jnp.zeros((slot_count, D), jnp.float32))
        (expert_out, expert_back), _ = lax.scan(block_step, start_totals, jnp.arange(block_count, dtype=jnp.int32))
        picked = jnp.minimum(target, slot_count - 1)
        weight_e = jnp.sum(jnp.where(routes == expert, router_gates, 0.0), axis=-1)
        chosen_flat = chosen.reshape(-1)
        outputs = outputs + jnp.where(chosen_flat[:, None], weight_e[:, None] * expert_out[picked], 0.0)
        grads = grads + jnp.where(chosen_flat[:, None], weight_e[:, None] * expert_back[picked], 0.0)
    return outputs.astype(jnp.bfloat16), grads.astype(jnp.bfloat16)
```

```python
import functools

import jax
import jax.numpy as jnp
from jax import lax
from jax.experimental import pallas as pl
from jax.experimental.pallas import tpu as pltpu
from jax.sharding import PartitionSpec as P

MESH = pl.DeviceIdType.MESH
BF = jnp.bfloat16
F32 = jnp.float32

EXPERTS = 4
NB = 8
NM = 16
TOK = 48
D = 8192
HID = 448
MAIN, TAIL = 384, 64
CH = 2 * HID
SLOTS = 15
PAD = 16
ROWS = SLOTS * NM
PROWS = PAD * NM
COLS = D // NM
OUTC = D // NB
KC = 512
NK = D // KC
WB = 3
HALF0 = 128


def dot(a, b):
    return jnp.dot(a, b, preferred_element_type=F32)


def dot_nt(a, b):
    return lax.dot_general(a, b, (((1,), (1,)), ((), ())), preferred_element_type=F32)


def to_slot_major():
    q = lax.broadcasted_iota(jnp.int32, (ROWS, PROWS), 0)
    r = lax.broadcasted_iota(jnp.int32, (ROWS, PROWS), 1)
    return (r == (q % 16) * 16 + q // 16).astype(F32).astype(BF)


def to_token_major():
    r = lax.broadcasted_iota(jnp.int32, (PROWS, ROWS), 0)
    q = lax.broadcasted_iota(jnp.int32, (PROWS, ROWS), 1)
    return (r == (q % 16) * 16 + q // 16).astype(F32).astype(BF)


class Net:
    def __init__(self, send_sem, recv_sem):
        self.send_sem, self.recv_sem = send_sem, recv_sem
        self.started = []

    def send(self, src, dst, device):
        k = len(self.started)
        copy = pltpu.make_async_remote_copy(
            src_ref=src,
            dst_ref=dst,
            send_sem=self.send_sem.at[k],
            recv_sem=self.recv_sem.at[k],
            device_id=device,
            device_id_type=MESH,
        )
        copy.start()
        self.started.append(copy)
        return copy


def row_half(ref, h):
    return ref.at[pl.ds(0, HALF0), :] if h == 0 else ref.at[pl.ds(HALF0, ROWS - HALF0), :]


def lane_half(ref, h):
    return ref.at[:, pl.ds(h * (D // 2), D // 2)]


def kernel(
    tokens, cots, table, comb, w_in, w_down,
    out_ref, back_ref, w_part,
    x_all, cot_send, cot_all, down, bp, ra_opp, ra, rb_opp, rb,
    act_all, wbuf, acc, pgate, pup, grads, ri_opp, ri, rj_opp, rj,
    out_acc, o_send, o_all, out_in, y_send, back_in,
    send_sem, recv_sem, lsem, wsem,
):
    branch = lax.axis_index("branch")
    me = lax.axis_index("mp")
    core = branch % 2
    s_a, s_b = 1 + 3 * core, 4 - 3 * core
    a0, b0 = (me // s_a) % 4, (me // s_b) % 4

    def at(da, db):
        return ((a0 + da + 4) % 4) * s_a + ((b0 + db + 4) % 4) * s_b

    def in_plane(da, db):
        return (branch, at(da, db))

    partner = (branch + 1 - 2 * core, me)
    net = Net(send_sem, recv_sem)

    barrier = pltpu.get_barrier_semaphore()

    def greet_plane(d, _):
        pl.semaphore_signal(barrier, inc=1, device_id=(branch, (me + d) % NM), device_id_type=MESH)
        return 0

    def greet_column(d, _):
        pl.semaphore_signal(barrier, inc=1, device_id=((branch + d) % NB, me), device_id_type=MESH)
        return 0

    lax.fori_loop(1, NM, greet_plane, 0)
    lax.fori_loop(1, NB, greet_column, 0)

    own_down = [
        pltpu.make_async_copy(w_down.at[:, pl.ds(0, MAIN), :], down.at[:, pl.ds(0, MAIN), :], lsem.at[0]),
        pltpu.make_async_copy(w_down.at[:, pl.ds(MAIN, TAIL), :], down.at[:, pl.ds(2 * MAIN, TAIL), :], lsem.at[1]),
    ]
    for c in own_down:
        c.start()

    pick = table[...]
    for g in range(NM):
        cols = slice(g * COLS, (g + 1) * COLS)
        cot_send[g] = dot(pick, cots[:, cols]).astype(BF)
    for g in range(NM):
        cols = slice(g * COLS, (g + 1) * COLS)
        x_all[me, :, cols] = dot(pick, tokens[:, cols]).astype(BF)
    cot_all[me] = cot_send[me]

    pl.semaphore_wait(barrier, NM - 1 + NB - 1)

    cot_copies = []
    for d in range(1, NM):
        to = (me + d) % NM
        cot_copies.append(net.send(cot_send.at[to], cot_all.at[me], (branch, to)))

    def gather_start(buf):
        return {
            "a": [net.send(buf.at[me], buf.at[me], in_plane(1, 0)), net.send(buf.at[me], buf.at[me], in_plane(-1, 0))],
            "b": [[net.send(buf.at[me], buf.at[me], in_plane(0, 1)), net.send(buf.at[me], buf.at[me], in_plane(0, -1))]],
        }

    def gather_a1(buf, st, half):
        st["h"] = []
        for i, da in ((0, -1), (1, 1)):
            st["a"][i].wait_recv()
            blk = buf.at[at(da, 0)]
            st["h"].append(net.send(half(blk, i), half(blk, i), in_plane(-da, 0)))
        for da in (-1, 1):
            blk = buf.at[at(da, 0)]
            st["b"].append([net.send(blk, blk, in_plane(0, 1)), net.send(blk, blk, in_plane(0, -1))])

    def gather_a2(buf, st):
        for h in st["h"]:
            h.wait_recv()
        blk = buf.at[at(2, 0)]
        st["b"].append([net.send(blk, blk, in_plane(0, 1)), net.send(blk, blk, in_plane(0, -1))])
        st["g"] = []

    def gather_b1(buf, st, half, n):
        da = (0, -1, 1, 2)[n]
        pair = []
        for i, db in ((0, -1), (1, 1)):
            st["b"][n][i].wait_recv()
            blk = buf.at[at(da, db)]
            pair.append(net.send(half(blk, i), half(blk, i), in_plane(0, -db)))
        st["g"].append(pair)

    def gather_b2(st, n):
        for g in st["g"][n]:
            g.wait_recv()

    ORDER = (2, 1, -1, 0)

    def reduce_a1(buf, opp, half, st):
        st["o"] = []
        for j, db in enumerate(ORDER):
            blk = buf.at[at(2, db)]
            st["o"].append([net.send(half(blk, 0), half(opp.at[0, j], 0), in_plane(1, 0)),
                            net.send(half(blk, 1), half(opp.at[1, j], 1), in_plane(-1, 0))])

    def reduce_a2(buf, acc_in, half, st):
        st["n"] = []
        for j, db in enumerate(ORDER):
            up, dn = buf.at[at(1, db)], buf.at[at(-1, db)]
            st["n"].append([net.send(half(up, 1), half(acc_in.at[0, j], 1), in_plane(1, 0)),
                            net.send(half(dn, 0), half(acc_in.at[1, j], 0), in_plane(-1, 0))])
        st["m"] = []

    def add_to(dst, src):
        dst[...] = (dst[...].astype(F32) + src[...].astype(F32)).astype(BF)

    def reduce_a3(buf, opp, acc_in, half, st, j):
        db = ORDER[j]
        pair = []
        for i, da in ((0, 1), (1, -1)):
            st["o"][j][i].wait_recv()
            blk = half(buf.at[at(da, db)], i)
            add_to(blk, half(opp.at[i, j], i))
            pair.append(net.send(blk, half(acc_in.at[i, j], i), in_plane(da, 0)))
        st["m"].append(pair)

    def reduce_a4(buf, acc_in, st, j):
        db = ORDER[j]
        for i in (0, 1):
            st["n"][j][i].wait_recv()
            st["m"][j][i].wait_recv()
        blk = buf.at[at(0, db)]
        blk[...] = (blk[...].astype(F32) + acc_in[0, j].astype(F32) + acc_in[1, j].astype(F32)).astype(BF)

    def reduce_b1(buf, opp, half, st):
        blk = buf.at[at(0, 2)]
        st["bo"] = [net.send(half(blk, 0), half(opp.at[0], 0), in_plane(0, 1)),
                    net.send(half(blk, 1), half(opp.at[1], 1), in_plane(0, -1))]

    def reduce_b2(buf, acc_in, half, st):
        up, dn = buf.at[at(0, 1)], buf.at[at(0, -1)]
        st["bn"] = [net.send(half(up, 1), half(acc_in.at[0], 1), in_plane(0, 1)),
                    net.send(half(dn, 0), half(acc_in.at[1], 0), in_plane(0, -1))]

    def reduce_b3(buf, opp, acc_in, half, st):
        st["bm"] = []
        for i, db in ((0, 1), (1, -1)):
            st["bo"][i].wait_recv()
            blk = half(buf.at[at(0, db)], i)
            add_to(blk, half(opp.at[i], i))
            st["bm"].append(net.send(blk, half(acc_in.at[i], i), in_plane(0, db)))

    def reduce_b4(st):
        for i in (0, 1):
            st["bn"][i].wait_recv()
            st["bm"][i].wait_recv()

    toks = gather_start(x_all)
    down_part = [
        net.send(w_down.at[:, pl.ds(0, MAIN), :], down.at[:, pl.ds(MAIN, MAIN), :], partner),
        net.send(w_down.at[:, pl.ds(MAIN, TAIL), :], down.at[:, pl.ds(2 * MAIN + TAIL, TAIL), :], partner),
    ]
    in_part = [net.send(w_in.at[g], w_part.at[g], partner) for g in range(2)]

    for c in cot_copies:
        c.wait_recv()
    cot_rows = dot(to_slot_major(), cot_all[...].reshape(PROWS, COLS)).astype(BF)

    gather_a1(x_all, toks, lane_half)

    for c in own_down:
        c.wait()
    for c in down_part:
        c.wait_recv()

    def partials(da):
        def one(j, _):
            m = at(da, j)
            bp[m] = dot_nt(cot_rows, down[m]).astype(BF)
            return 0

        lax.fori_loop(0, 4, one, 0)

    rs = {}
    partials(2)
    reduce_a1(bp, ra_opp, row_half, rs)
    gather_a2(x_all, toks)
    partials(1)
    partials(-1)
    reduce_a2(bp, ra, row_half, rs)
    for n in range(4):
        gather_b1(x_all, toks, lane_half, n)
    partials(0)
    for j in range(4):
        reduce_a3(bp, ra_opp, ra, row_half, rs, j)
    for n in range(4):
        gather_b2(toks, n)
    for c in in_part:
        c.wait_recv()

    def tiles(i, slot):
        rows = pl.ds(pl.multiple_of(i * KC, KC), KC)
        return [
            pltpu.make_async_copy((w_in if w < 2 else w_part).at[w % 2, rows, :], wbuf.at[slot, w], wsem.at[slot, w])
            for w in range(4)
        ]

    def prime():
        for i in range(WB - 1):
            for c in tiles(i, i):
                c.start()

    def stream(lo, hi, body):
        def one(i, _):
            @pl.when(i + WB - 1 < NK)
            def _():
                for c in tiles(i + WB - 1, (i + WB - 1) % WB):
                    c.start()

            slot = i % WB
            for c in tiles(i, slot):
                c.wait()
            body(i, slot)
            return 0

        lax.fori_loop(lo, hi, one, 0)

    acc[...] = jnp.zeros_like(acc)

    def forward(i, slot):
        cols = pl.ds(pl.multiple_of(i * KC, KC), KC)
        rows = dot(to_slot_major(), x_all[:, :, cols].reshape(PROWS, KC)).astype(BF)
        for w in range(4):
            acc[w] += dot(rows, wbuf[slot, w])

    prime()
    stream(0, 6, forward)
    for j in range(3):
        reduce_a4(bp, ra, rs, j)
        if j == 0:
            reduce_b1(bp, rb_opp, row_half, rs)
    reduce_b2(bp, rb, row_half, rs)
    stream(6, 12, forward)
    reduce_a4(bp, ra, rs, 3)
    reduce_b3(bp, rb_opp, rb, row_half, rs)
    stream(12, NK, forward)

    for dst, w in ((pgate, 0), (pup, 1)):
        dst[:, 0:MAIN] = acc[w, :, 0:MAIN]
        dst[:, MAIN : 2 * MAIN] = acc[w + 2, :, 0:MAIN]
        dst[:, 2 * MAIN : CH] = jnp.concatenate([acc[w, :, MAIN:HID], acc[w + 2, :, MAIN:HID]], axis=1)

    def activate(i, _):
        r = pl.ds(pl.multiple_of(i * 16, 16), 16)
        g = pgate[r, :]
        s = 1.0 / (1.0 + jnp.exp(-g))
        act_all[me, r, :] = (g * s * pup[r, :]).astype(BF)
        return 0

    lax.fori_loop(0, SLOTS, activate, 0)
    acts = gather_start(act_all)

    reduce_b4(rs)

    def gradients(i, _):
        r = pl.ds(pl.multiple_of(i * 16, 16), 16)
        h = bp[me, r, :].astype(F32) + rb[0, r, :].astype(F32) + rb[1, r, :].astype(F32)
        g, u = pgate[r, :], pup[r, :]
        s = 1.0 / (1.0 + jnp.exp(-g))
        pgate[r, :] = h * u * s * (1.0 + g * (1.0 - s))
        pup[r, :] = h * g * s
        return 0

    lax.fori_loop(0, SLOTS, gradients, 0)
    for src, w in ((pgate, 0), (pup, 1)):
        moved = dot(to_token_major(), src[...].astype(BF))
        grads[w, :, 0:MAIN] = moved[:, 0:MAIN].astype(BF)
        grads[w + 2, :, 0:MAIN] = moved[:, MAIN : 2 * MAIN].astype(BF)
        grads[w, :, MAIN:HID] = moved[:, 2 * MAIN : 2 * MAIN + TAIL].astype(BF)
        grads[w + 2, :, MAIN:HID] = moved[:, 2 * MAIN + TAIL : CH].astype(BF)

    gather_a1(act_all, acts, row_half)

    for c in toks["a"] + toks["h"] + sum(toks["b"], []) + sum(toks["g"], []):
        c.wait_send()

    def backward(i, slot):
        cols = pl.ds(pl.multiple_of(i * KC, KC), KC)
        total = dot_nt(grads[0], wbuf[slot, 0])
        for w in range(1, 4):
            total += dot_nt(grads[w], wbuf[slot, w])
        x_all[:, :, cols] = total.astype(BF).reshape(NM, PAD, KC)

    prime()
    stream(0, 6, backward)
    gather_a2(act_all, acts)
    for n in range(2):
        gather_b1(act_all, acts, row_half, n)
    stream(6, 12, backward)
    gather_b1(act_all, acts, row_half, 2)
    stream(12, NK, backward)

    ri_st = {}
    reduce_a1(x_all, ri_opp, lane_half, ri_st)
    reduce_a2(x_all, ri, lane_half, ri_st)
    gather_b1(act_all, acts, row_half, 3)

    def outs(da, db):
        m = at(da, db)
        return dot(act_all[m], down[m])

    out_acc[...] = outs(0, 0)
    for da, db in ((-1, 0), (1, 0), (2, 0)):
        out_acc[...] += outs(da, db)
    for j in range(4):
        reduce_a3(x_all, ri_opp, ri, lane_half, ri_st, j)
    for da in (0, -1, 1, 2):
        for db in (-1, 1):
            out_acc[...] += outs(da, db)
    for j in range(4):
        reduce_a4(x_all, ri, ri_st, j)
        if j == 0:
            reduce_b1(x_all, rj_opp, lane_half, ri_st)
        if j == 2:
            reduce_b2(x_all, rj, lane_half, ri_st)
    for n, da in enumerate((0, -1, 1, 2)):
        gather_b2(acts, n)
        out_acc[...] += outs(da, 2)
    o_send[...] = dot(to_token_major(), out_acc[...].astype(BF)).astype(BF).reshape(NM, PAD, COLS)
    o_all[me] = o_send[me]
    o_copies = []
    for d in range(1, NM):
        to = (me + d) % NM
        o_copies.append(net.send(o_send.at[to], o_all.at[me], (branch, to)))
    reduce_b3(x_all, rj_opp, rj, lane_half, ri_st)
    for c in o_copies:
        c.wait_recv()
    out_in[branch] = o_all[pl.ds(2 * branch, 2)]
    finals = []
    for d in range(1, NB):
        to = (branch + d) % NB
        finals.append(net.send(o_all.at[pl.ds(2 * to, 2)], out_in.at[branch], (to, me)))
    reduce_b4(ri_st)
    for g in range(NB):
        cols = slice(g * OUTC, (g + 1) * OUTC)
        y_send[g] = (
            x_all[me, :, cols].astype(F32) + rj[0, :, cols].astype(F32) + rj[1, :, cols].astype(F32)
        ).astype(BF)
    back_in[branch] = y_send[branch]
    for d in range(1, NB):
        to = (branch + d) % NB
        finals.append(net.send(y_send.at[to], back_in.at[branch], (to, me)))

    weights = comb[...]
    hi = weights.astype(BF)
    lo = (weights - hi.astype(F32)).astype(BF)
    for c in finals[: NB - 1]:
        c.wait_recv()
    for j in range(2):
        got = out_in[:, j].reshape(NB * PAD, COLS)
        out_ref[:, j * COLS : (j + 1) * COLS] = (dot(hi, got) + dot(lo, got)).astype(BF)
    for c in finals[NB - 1 :]:
        c.wait_recv()
    got = back_in[...].reshape(NB * PAD, OUTC)
    back_ref[...] = (dot(hi, got) + dot(lo, got)).astype(BF)

    reused = toks["a"] + toks["h"] + sum(toks["b"], []) + sum(toks["g"], [])
    for c in net.started:
        if not any(c is r for r in reused):
            c.wait_send()


N_COPIES = 200


def on_device(tokens, cotangent, routes, router_gates, expert_in, expert_down):
    branch = lax.axis_index("branch")
    expert, core = branch // 2, branch % 2
    named = routes[:, :, None] == jnp.arange(EXPERTS, dtype=jnp.int32)
    chosen = jnp.any(named, axis=1)
    counted = chosen.astype(jnp.int32)
    places = jnp.cumsum(counted, axis=0) - counted
    mine = jnp.arange(EXPERTS, dtype=jnp.int32) == expert
    own_place = jnp.sum(jnp.where(jnp.logical_and(mine, chosen), places + 1, 0), axis=1) - 1
    spots = jnp.arange(PAD, dtype=jnp.int32)
    wanted = jnp.where(spots < SLOTS, core * SLOTS + spots, -2)
    table = (wanted[:, None] == own_place[None, :]).astype(BF)
    gates = jnp.sum(jnp.where(named, router_gates[:, :, None], 0.0), axis=1)
    column = jnp.arange(NB * PAD, dtype=jnp.int32)
    col_slot = jnp.where(column % PAD < SLOTS, (column // PAD % 2) * SLOTS + column % PAD, -2)
    col_expert = column // (2 * PAD)
    comb = jnp.zeros((TOK, NB * PAD), F32)
    for e in range(EXPERTS):
        hit = jnp.logical_and(col_expert[None, :] == e, col_slot[None, :] == places[:, e : e + 1])
        comb += jnp.where(hit, gates[:, e : e + 1], 0.0)

    vm = pl.BlockSpec(memory_space=pltpu.VMEM)
    hbm = pl.BlockSpec(memory_space=pl.ANY)
    out, back, _ = pl.pallas_call(
        kernel,
        out_shape=(
            jax.ShapeDtypeStruct((TOK, OUTC), BF),
            jax.ShapeDtypeStruct((TOK, OUTC), BF),
            jax.ShapeDtypeStruct((2, D, HID), BF),
        ),
        in_specs=[vm, vm, vm, vm, hbm, hbm],
        out_specs=(vm, vm, hbm),
        scratch_shapes=[
            pltpu.VMEM((NM, PAD, D), BF),
            pltpu.VMEM((NM, PAD, COLS), BF),
            pltpu.VMEM((NM, PAD, COLS), BF),
            pltpu.VMEM((NM, CH, COLS), BF),
            pltpu.VMEM((NM, ROWS, CH), BF),
            pltpu.VMEM((2, 4, ROWS, CH), BF),
            pltpu.VMEM((2, 4, ROWS, CH), BF),
            pltpu.VMEM((2, ROWS, CH), BF),
            pltpu.VMEM((2, ROWS, CH), BF),
            pltpu.VMEM((NM, ROWS, CH), BF),
            pltpu.VMEM((WB, 4, KC, HID), BF),
            pltpu.VMEM((4, ROWS, HID), F32),
            pltpu.VMEM((ROWS, CH), F32),
            pltpu.VMEM((ROWS, CH), F32),
            pltpu.VMEM((4, PROWS, HID), BF),
            pltpu.VMEM((2, 4, PAD, D), BF),
            pltpu.VMEM((2, 4, PAD, D), BF),
            pltpu.VMEM((2, PAD, D), BF),
            pltpu.VMEM((2, PAD, D), BF),
            pltpu.VMEM((ROWS, COLS), F32),
            pltpu.VMEM((NM, PAD, COLS), BF),
            pltpu.VMEM((NM, PAD, COLS), BF),
            pltpu.VMEM((NB, 2, PAD, COLS), BF),
            pltpu.VMEM((NB, PAD, OUTC), BF),
            pltpu.VMEM((NB, PAD, OUTC), BF),
            pltpu.SemaphoreType.DMA((N_COPIES,)),
            pltpu.SemaphoreType.DMA((N_COPIES,)),
            pltpu.SemaphoreType.DMA((2,)),
            pltpu.SemaphoreType.DMA((WB, 4)),
        ],
        compiler_params=pltpu.CompilerParams(
            collective_id=0, has_side_effects=True, vmem_limit_bytes=66060288
        ),
        name="expert_step",
    )(tokens, cotangent, table, comb, expert_in, expert_down.reshape(NM, HID, COLS))
    return out, back


def solution(mesh):
    placed = (
        P("mp", None),
        P("mp", None),
        P("mp", None),
        P("mp", None),
        P(None, None, ("branch", "mp")),
        P("branch", "mp"),
    )
    return jax.shard_map(
        on_device,
        mesh=mesh,
        in_specs=placed,
        out_specs=(P("mp", "branch"), P("mp", "branch")),
        check_vma=False,
    )
```

```python
import functools

import jax
import jax.numpy as jnp
from jax import lax
from jax.experimental import pallas as pl
from jax.experimental.pallas import tpu as pltpu
from jax.sharding import PartitionSpec as P

MESH = pl.DeviceIdType.MESH
BF = jnp.bfloat16
F32 = jnp.float32

EXPERTS = 4
NB = 8
NM = 16
TOK = 48
D = 8192
HID = 448
CH = 2 * HID
SLOTS = 15
PAD = 16
ROWS = SLOTS * NM
PROWS = PAD * NM
COLS = D // NM
OUTC = D // NB
KC = 512
NK = D // KC
WB = 3
HALF0 = 128


def dot(a, b):
    return jnp.dot(a, b, preferred_element_type=F32)


def dot_nt(a, b):
    return lax.dot_general(a, b, (((1,), (1,)), ((), ())), preferred_element_type=F32)


def to_slot_major():
    q = lax.broadcasted_iota(jnp.int32, (ROWS, PROWS), 0)
    r = lax.broadcasted_iota(jnp.int32, (ROWS, PROWS), 1)
    return (r == (q % 16) * 16 + q // 16).astype(F32).astype(BF)


def to_token_major():
    r = lax.broadcasted_iota(jnp.int32, (PROWS, ROWS), 0)
    q = lax.broadcasted_iota(jnp.int32, (PROWS, ROWS), 1)
    return (r == (q % 16) * 16 + q // 16).astype(F32).astype(BF)


class Net:
    def __init__(self, send_sem, recv_sem):
        self.send_sem, self.recv_sem = send_sem, recv_sem
        self.started = []

    def send(self, src, dst, device):
        k = len(self.started)
        copy = pltpu.make_async_remote_copy(
            src_ref=src,
            dst_ref=dst,
            send_sem=self.send_sem.at[k],
            recv_sem=self.recv_sem.at[k],
            device_id=device,
            device_id_type=MESH,
        )
        copy.start()
        self.started.append(copy)
        return copy


def row_half(ref, h):
    return ref.at[pl.ds(0, HALF0), :] if h == 0 else ref.at[pl.ds(HALF0, ROWS - HALF0), :]


def lane_half(ref, h):
    return ref.at[:, pl.ds(h * (D // 2), D // 2)]


def kernel(
    tokens, cots, table, comb, w_in, w_down,
    out_ref, back_ref, w_part,
    x_all, cot_send, cot_all, down, bp, ra_opp, ra, rb_opp, rb,
    act_all, wbuf, pgate, pup, grads, ri_opp, ri, rj_opp, rj,
    out_acc, o_send, o_all, out_in, y_send, back_in,
    send_sem, recv_sem, lsem, wsem,
):
    branch = lax.axis_index("branch")
    me = lax.axis_index("mp")
    core = branch % 2
    s_a, s_b = 1 + 3 * core, 4 - 3 * core
    a0, b0 = (me // s_a) % 4, (me // s_b) % 4

    def at(da, db):
        return ((a0 + da + 4) % 4) * s_a + ((b0 + db + 4) % 4) * s_b

    def in_plane(da, db):
        return (branch, at(da, db))

    partner = (branch + 1 - 2 * core, me)
    net = Net(send_sem, recv_sem)

    barrier = pltpu.get_barrier_semaphore()

    def greet_plane(d, _):
        pl.semaphore_signal(barrier, inc=1, device_id=(branch, (me + d) % NM), device_id_type=MESH)
        return 0

    def greet_column(d, _):
        pl.semaphore_signal(barrier, inc=1, device_id=((branch + d) % NB, me), device_id_type=MESH)
        return 0

    lax.fori_loop(1, NM, greet_plane, 0)
    lax.fori_loop(1, NB, greet_column, 0)

    own_down = pltpu.make_async_copy(w_down, down.at[:, pl.ds(0, HID), :], lsem)
    own_down.start()

    pick = table[...]
    for g in range(NM):
        cols = slice(g * COLS, (g + 1) * COLS)
        cot_send[g] = dot(pick, cots[:, cols]).astype(BF)
    for g in range(NM):
        cols = slice(g * COLS, (g + 1) * COLS)
        x_all[me, :, cols] = dot(pick, tokens[:, cols]).astype(BF)
    cot_all[me] = cot_send[me]

    pl.semaphore_wait(barrier, NM - 1 + NB - 1)

    cot_copies = []
    for d in range(1, NM):
        to = (me + d) % NM
        cot_copies.append(net.send(cot_send.at[to], cot_all.at[me], (branch, to)))

    def gather_start(buf):
        return {
            "a": [net.send(buf.at[me], buf.at[me], in_plane(1, 0)), net.send(buf.at[me], buf.at[me], in_plane(-1, 0))],
            "b": [[net.send(buf.at[me], buf.at[me], in_plane(0, 1)), net.send(buf.at[me], buf.at[me], in_plane(0, -1))]],
        }

    def gather_a1(buf, st, half):
        st["h"] = []
        for i, da in ((0, -1), (1, 1)):
            st["a"][i].wait_recv()
            blk = buf.at[at(da, 0)]
            st["h"].append(net.send(half(blk, i), half(blk, i), in_plane(-da, 0)))
        for da in (-1, 1):
            blk = buf.at[at(da, 0)]
            st["b"].append([net.send(blk, blk, in_plane(0, 1)), net.send(blk, blk, in_plane(0, -1))])

    def gather_a2(buf, st):
        for h in st["h"]:
            h.wait_recv()
        blk = buf.at[at(2, 0)]
        st["b"].append([net.send(blk, blk, in_plane(0, 1)), net.send(blk, blk, in_plane(0, -1))])
        st["g"] = []

    def gather_b1(buf, st, half, n):
        da = (0, -1, 1, 2)[n]
        pair = []
        for i, db in ((0, -1), (1, 1)):
            st["b"][n][i].wait_recv()
            blk = buf.at[at(da, db)]
            pair.append(net.send(half(blk, i), half(blk, i), in_plane(0, -db)))
        st["g"].append(pair)

    def gather_b2(st, n):
        for g in st["g"][n]:
            g.wait_recv()

    ORDER = (2, 1, -1, 0)

    def reduce_a1(buf, opp, half, st):
        st["o"] = []
        for j, db in enumerate(ORDER):
            blk = buf.at[at(2, db)]
            st["o"].append([net.send(half(blk, 0), half(opp.at[0, j], 0), in_plane(1, 0)),
                            net.send(half(blk, 1), half(opp.at[1, j], 1), in_plane(-1, 0))])

    def reduce_a2(buf, acc_in, half, st):
        st["n"] = []
        for j, db in enumerate(ORDER):
            up, dn = buf.at[at(1, db)], buf.at[at(-1, db)]
            st["n"].append([net.send(half(up, 1), half(acc_in.at[0, j], 1), in_plane(1, 0)),
                            net.send(half(dn, 0), half(acc_in.at[1, j], 0), in_plane(-1, 0))])
        st["m"] = []

    def add_to(dst, src):
        dst[...] = (dst[...].astype(F32) + src[...].astype(F32)).astype(BF)

    def reduce_a3(buf, opp, acc_in, half, st, j):
        db = ORDER[j]
        pair = []
        for i, da in ((0, 1), (1, -1)):
            st["o"][j][i].wait_recv()
            blk = half(buf.at[at(da, db)], i)
            add_to(blk, half(opp.at[i, j], i))
            pair.append(net.send(blk, half(acc_in.at[i, j], i), in_plane(da, 0)))
        st["m"].append(pair)

    def reduce_a4(buf, acc_in, st, j):
        db = ORDER[j]
        for i in (0, 1):
            st["n"][j][i].wait_recv()
            st["m"][j][i].wait_recv()
        blk = buf.at[at(0, db)]
        blk[...] = (blk[...].astype(F32) + acc_in[0, j].astype(F32) + acc_in[1, j].astype(F32)).astype(BF)

    def reduce_b1(buf, opp, half, st):
        blk = buf.at[at(0, 2)]
        st["bo"] = [net.send(half(blk, 0), half(opp.at[0], 0), in_plane(0, 1)),
                    net.send(half(blk, 1), half(opp.at[1], 1), in_plane(0, -1))]

    def reduce_b2(buf, acc_in, half, st):
        up, dn = buf.at[at(0, 1)], buf.at[at(0, -1)]
        st["bn"] = [net.send(half(up, 1), half(acc_in.at[0], 1), in_plane(0, 1)),
                    net.send(half(dn, 0), half(acc_in.at[1], 0), in_plane(0, -1))]

    def reduce_b3(buf, opp, acc_in, half, st):
        st["bm"] = []
        for i, db in ((0, 1), (1, -1)):
            st["bo"][i].wait_recv()
            blk = half(buf.at[at(0, db)], i)
            add_to(blk, half(opp.at[i], i))
            st["bm"].append(net.send(blk, half(acc_in.at[i], i), in_plane(0, db)))

    def reduce_b4(st):
        for i in (0, 1):
            st["bn"][i].wait_recv()
            st["bm"][i].wait_recv()

    toks = gather_start(x_all)
    down_part = net.send(w_down, down.at[:, pl.ds(HID, HID), :], partner)
    in_part = [net.send(w_in.at[g], w_part.at[g], partner) for g in range(2)]

    for c in cot_copies:
        c.wait_recv()
    cot_rows = dot(to_slot_major(), cot_all[...].reshape(PROWS, COLS)).astype(BF)

    gather_a1(x_all, toks, lane_half)

    own_down.wait()
    down_part.wait_recv()

    def partials(da):
        def one(j, _):
            m = at(da, j)
            bp[m] = dot_nt(cot_rows, down[m]).astype(BF)
            return 0

        lax.fori_loop(0, 4, one, 0)

    rs = {}
    partials(2)
    reduce_a1(bp, ra_opp, row_half, rs)
    gather_a2(x_all, toks)
    partials(1)
    partials(-1)
    reduce_a2(bp, ra, row_half, rs)
    for n in range(4):
        gather_b1(x_all, toks, lane_half, n)
    partials(0)
    for j in range(4):
        reduce_a3(bp, ra_opp, ra, row_half, rs, j)
    for n in range(4):
        gather_b2(toks, n)
    for c in in_part:
        c.wait_recv()

    def tiles(i, slot):
        cols = pl.ds(pl.multiple_of(i * KC, KC), KC)
        return [
            pltpu.make_async_copy(src.at[g, :, cols], wbuf.at[slot, g, pl.ds(o * HID, HID), :], wsem.at[slot, g, o])
            for o, src in enumerate((w_in, w_part))
            for g in range(2)
        ]

    def prime():
        for i in range(WB - 1):
            for c in tiles(i, i):
                c.start()

    def stream(lo, hi, body):
        def one(i, _):
            @pl.when(i + WB - 1 < NK)
            def _():
                for c in tiles(i + WB - 1, (i + WB - 1) % WB):
                    c.start()

            slot = i % WB
            for c in tiles(i, slot):
                c.wait()
            body(i, slot)
            return 0

        lax.fori_loop(lo, hi, one, 0)

    pgate[...] = jnp.zeros_like(pgate)
    pup[...] = jnp.zeros_like(pup)

    def forward(i, slot):
        cols = pl.ds(pl.multiple_of(i * KC, KC), KC)
        rows = dot(to_slot_major(), x_all[:, :, cols].reshape(PROWS, KC)).astype(BF)
        pgate[...] += dot_nt(rows, wbuf[slot, 0])
        pup[...] += dot_nt(rows, wbuf[slot, 1])

    prime()
    stream(0, 6, forward)
    for j in range(3):
        reduce_a4(bp, ra, rs, j)
        if j == 0:
            reduce_b1(bp, rb_opp, row_half, rs)
    reduce_b2(bp, rb, row_half, rs)
    stream(6, 12, forward)
    reduce_a4(bp, ra, rs, 3)
    reduce_b3(bp, rb_opp, rb, row_half, rs)
    stream(12, NK, forward)

    def activate(i, _):
        r = pl.ds(pl.multiple_of(i * 16, 16), 16)
        g = pgate[r, :]
        s = 1.0 / (1.0 + jnp.exp(-g))
        act_all[me, r, :] = (g * s * pup[r, :]).astype(BF)
        return 0

    lax.fori_loop(0, SLOTS, activate, 0)
    acts = gather_start(act_all)

    reduce_b4(rs)

    def gradients(i, _):
        r = pl.ds(pl.multiple_of(i * 16, 16), 16)
        h = bp[me, r, :].astype(F32) + rb[0, r, :].astype(F32) + rb[1, r, :].astype(F32)
        g, u = pgate[r, :], pup[r, :]
        s = 1.0 / (1.0 + jnp.exp(-g))
        pgate[r, :] = h * u * s * (1.0 + g * (1.0 - s))
        pup[r, :] = h * g * s
        return 0

    lax.fori_loop(0, SLOTS, gradients, 0)
    for w, src in enumerate((pgate, pup)):
        grads[w] = dot(to_token_major(), src[...].astype(BF)).astype(BF)

    gather_a1(act_all, acts, row_half)

    for c in toks["a"] + toks["h"] + sum(toks["b"], []) + sum(toks["g"], []):
        c.wait_send()

    def backward(i, slot):
        cols = pl.ds(pl.multiple_of(i * KC, KC), KC)
        total = dot(grads[0], wbuf[slot, 0]) + dot(grads[1], wbuf[slot, 1])
        x_all[:, :, cols] = total.astype(BF).reshape(NM, PAD, KC)

    prime()
    stream(0, 6, backward)
    gather_a2(act_all, acts)
    for n in range(2):
        gather_b1(act_all, acts, row_half, n)
    stream(6, 12, backward)
    gather_b1(act_all, acts, row_half, 2)
    stream(12, NK, backward)

    ri_st = {}
    reduce_a1(x_all, ri_opp, lane_half, ri_st)
    reduce_a2(x_all, ri, lane_half, ri_st)
    gather_b1(act_all, acts, row_half, 3)

    def outs(da, db):
        m = at(da, db)
        return dot(act_all[m], down[m])

    out_acc[...] = outs(0, 0)
    for da, db in ((-1, 0), (1, 0), (2, 0)):
        out_acc[...] += outs(da, db)
    for j in range(4):
        reduce_a3(x_all, ri_opp, ri, lane_half, ri_st, j)
    for da in (0, -1, 1, 2):
        for db in (-1, 1):
            out_acc[...] += outs(da, db)
    for j in range(4):
        reduce_a4(x_all, ri, ri_st, j)
        if j == 0:
            reduce_b1(x_all, rj_opp, lane_half, ri_st)
        if j == 2:
            reduce_b2(x_all, rj, lane_half, ri_st)
    for n, da in enumerate((0, -1, 1, 2)):
        gather_b2(acts, n)
        out_acc[...] += outs(da, 2)
    o_send[...] = dot(to_token_major(), out_acc[...].astype(BF)).astype(BF).reshape(NM, PAD, COLS)
    o_all[me] = o_send[me]
    o_copies = []
    for d in range(1, NM):
        to = (me + d) % NM
        o_copies.append(net.send(o_send.at[to], o_all.at[me], (branch, to)))
    reduce_b3(x_all, rj_opp, rj, lane_half, ri_st)
    for c in o_copies:
        c.wait_recv()
    out_in[branch] = o_all[pl.ds(2 * branch, 2)]
    finals = []
    for d in range(1, NB):
        to = (branch + d) % NB
        finals.append(net.send(o_all.at[pl.ds(2 * to, 2)], out_in.at[branch], (to, me)))
    reduce_b4(ri_st)
    for g in range(NB):
        cols = slice(g * OUTC, (g + 1) * OUTC)
        y_send[g] = (
            x_all[me, :, cols].astype(F32) + rj[0, :, cols].astype(F32) + rj[1, :, cols].astype(F32)
        ).astype(BF)
    back_in[branch] = y_send[branch]
    for d in range(1, NB):
        to = (branch + d) % NB
        finals.append(net.send(y_send.at[to], back_in.at[branch], (to, me)))

    weights = comb[...]
    hi = weights.astype(BF)
    lo = (weights - hi.astype(F32)).astype(BF)
    for c in finals[: NB - 1]:
        c.wait_recv()
    for j in range(2):
        got = out_in[:, j].reshape(NB * PAD, COLS)
        out_ref[:, j * COLS : (j + 1) * COLS] = (dot(hi, got) + dot(lo, got)).astype(BF)
    for c in finals[NB - 1 :]:
        c.wait_recv()
    got = back_in[...].reshape(NB * PAD, OUTC)
    back_ref[...] = (dot(hi, got) + dot(lo, got)).astype(BF)

    reused = toks["a"] + toks["h"] + sum(toks["b"], []) + sum(toks["g"], [])
    for c in net.started:
        if not any(c is r for r in reused):
            c.wait_send()


N_COPIES = 200


def on_device(tokens, cotangent, routes, router_gates, expert_in, expert_down):
    branch = lax.axis_index("branch")
    expert, core = branch // 2, branch % 2
    named = routes[:, :, None] == jnp.arange(EXPERTS, dtype=jnp.int32)
    chosen = jnp.any(named, axis=1)
    counted = chosen.astype(jnp.int32)
    places = jnp.cumsum(counted, axis=0) - counted
    mine = jnp.arange(EXPERTS, dtype=jnp.int32) == expert
    own_place = jnp.sum(jnp.where(jnp.logical_and(mine, chosen), places + 1, 0), axis=1) - 1
    spots = jnp.arange(PAD, dtype=jnp.int32)
    wanted = jnp.where(spots < SLOTS, core * SLOTS + spots, -2)
    table = (wanted[:, None] == own_place[None, :]).astype(BF)
    gates = jnp.sum(jnp.where(named, router_gates[:, :, None], 0.0), axis=1)
    column = jnp.arange(NB * PAD, dtype=jnp.int32)
    col_slot = jnp.where(column % PAD < SLOTS, (column // PAD % 2) * SLOTS + column % PAD, -2)
    col_expert = column // (2 * PAD)
    comb = jnp.zeros((TOK, NB * PAD), F32)
    for e in range(EXPERTS):
        hit = jnp.logical_and(col_expert[None, :] == e, col_slot[None, :] == places[:, e : e + 1])
        comb += jnp.where(hit, gates[:, e : e + 1], 0.0)

    vm = pl.BlockSpec(memory_space=pltpu.VMEM)
    hbm = pl.BlockSpec(memory_space=pl.ANY)
    out, back, _ = pl.pallas_call(
        kernel,
        out_shape=(
            jax.ShapeDtypeStruct((TOK, OUTC), BF),
            jax.ShapeDtypeStruct((TOK, OUTC), BF),
            jax.ShapeDtypeStruct((2, HID, D), BF),
        ),
        in_specs=[vm, vm, vm, vm, hbm, hbm],
        out_specs=(vm, vm, hbm),
        scratch_shapes=[
            pltpu.VMEM((NM, PAD, D), BF),
            pltpu.VMEM((NM, PAD, COLS), BF),
            pltpu.VMEM((NM, PAD, COLS), BF),
            pltpu.VMEM((NM, CH, COLS), BF),
            pltpu.VMEM((NM, ROWS, CH), BF),
            pltpu.VMEM((2, 4, ROWS, CH), BF),
            pltpu.VMEM((2, 4, ROWS, CH), BF),
            pltpu.VMEM((2, ROWS, CH), BF),
            pltpu.VMEM((2, ROWS, CH), BF),
            pltpu.VMEM((NM, ROWS, CH), BF),
            pltpu.VMEM((WB, 2, CH, KC), BF),
            pltpu.VMEM((ROWS, CH), F32),
            pltpu.VMEM((ROWS, CH), F32),
            pltpu.VMEM((2, PROWS, CH), BF),
            pltpu.VMEM((2, 4, PAD, D), BF),
            pltpu.VMEM((2, 4, PAD, D), BF),
            pltpu.VMEM((2, PAD, D), BF),
            pltpu.VMEM((2, PAD, D), BF),
            pltpu.VMEM((ROWS, COLS), F32),
            pltpu.VMEM((NM, PAD, COLS), BF),
            pltpu.VMEM((NM, PAD, COLS), BF),
            pltpu.VMEM((NB, 2, PAD, COLS), BF),
            pltpu.VMEM((NB, PAD, OUTC), BF),
            pltpu.VMEM((NB, PAD, OUTC), BF),
            pltpu.SemaphoreType.DMA((N_COPIES,)),
            pltpu.SemaphoreType.DMA((N_COPIES,)),
            pltpu.SemaphoreType.DMA,
            pltpu.SemaphoreType.DMA((WB, 2, 2)),
        ],
        compiler_params=pltpu.CompilerParams(
            collective_id=0, has_side_effects=True, vmem_limit_bytes=66060288
        ),
        name="expert_step",
    )(tokens, cotangent, table, comb, expert_in.transpose(0, 2, 1), expert_down.reshape(NM, HID, COLS))
    return out, back


def solution(mesh):
    placed = (
        P("mp", None),
        P("mp", None),
        P("mp", None),
        P("mp", None),
        P(None, None, ("branch", "mp")),
        P("branch", "mp"),
    )
    return jax.shard_map(
        on_device,
        mesh=mesh,
        in_specs=placed,
        out_specs=(P("mp", "branch"), P("mp", "branch")),
        check_vma=False,
    )
```

```python
import functools

import jax
import jax.numpy as jnp
from jax import lax
from jax.experimental import pallas as pl
from jax.experimental.pallas import tpu as pltpu
from jax.sharding import PartitionSpec as P

MESH = pl.DeviceIdType.MESH
BF = jnp.bfloat16
F32 = jnp.float32

EXPERTS = 4
NB = 8
NM = 16
TOK = 48
D = 8192
HID = 448
CH = 2 * HID
SLOTS = 15
PAD = 16
ROWS = SLOTS * NM
PROWS = PAD * NM
COLS = D // NM
OUTC = D // NB
KC = 1024
NK = D // KC
WB = 2
HALF0 = 128


def dot(a, b):
    return jnp.dot(a, b, preferred_element_type=F32)


def dot_nt(a, b):
    return lax.dot_general(a, b, (((1,), (1,)), ((), ())), preferred_element_type=F32)


def to_slot_major():
    q = lax.broadcasted_iota(jnp.int32, (ROWS, PROWS), 0)
    r = lax.broadcasted_iota(jnp.int32, (ROWS, PROWS), 1)
    return (r == (q % 16) * 16 + q // 16).astype(F32).astype(BF)


def to_token_major():
    r = lax.broadcasted_iota(jnp.int32, (PROWS, ROWS), 0)
    q = lax.broadcasted_iota(jnp.int32, (PROWS, ROWS), 1)
    return (r == (q % 16) * 16 + q // 16).astype(F32).astype(BF)


class Net:
    def __init__(self, send_sem, recv_sem):
        self.send_sem, self.recv_sem = send_sem, recv_sem
        self.started = []

    def send(self, src, dst, device):
        k = len(self.started)
        copy = pltpu.make_async_remote_copy(
            src_ref=src,
            dst_ref=dst,
            send_sem=self.send_sem.at[k],
            recv_sem=self.recv_sem.at[k],
            device_id=device,
            device_id_type=MESH,
        )
        copy.start()
        self.started.append(copy)
        return copy


def row_half(ref, h):
    return ref.at[pl.ds(0, HALF0), :] if h == 0 else ref.at[pl.ds(HALF0, ROWS - HALF0), :]


def whole(ref):
    return ref


def lane_half(ref, h):
    return ref.at[:, pl.ds(h * (D // 2), D // 2)]


def kernel(
    tokens, cots, routes, gates, w_in, w_down,
    out_ref, back_ref, w_part,
    x_all, cot_send, cot_all, down, bp, ra_opp, ra, rb_opp, rb,
    act_all, wbuf, pgate, pup, grads, ri_opp, ri, rj_opp, rj,
    out_acc, o_send, o_all, out_in, y_send, back_in, comb,
    send_sem, recv_sem, lsem, wsem,
):
    branch = lax.axis_index("branch")
    me = lax.axis_index("mp")
    core = branch % 2
    s_a, s_b = 1 + 3 * core, 4 - 3 * core
    a0, b0 = (me // s_a) % 4, (me // s_b) % 4

    def at(da, db):
        return ((a0 + da + 4) % 4) * s_a + ((b0 + db + 4) % 4) * s_b

    def in_plane(da, db):
        return (branch, at(da, db))

    partner = (branch + 1 - 2 * core, me)
    net = Net(send_sem, recv_sem)

    barrier = pltpu.get_barrier_semaphore()

    def greet_plane(d, _):
        pl.semaphore_signal(barrier, inc=1, device_id=(branch, (me + d) % NM), device_id_type=MESH)
        return 0

    def greet_column(d, _):
        pl.semaphore_signal(barrier, inc=1, device_id=((branch + d) % NB, me), device_id_type=MESH)
        return 0

    lax.fori_loop(1, NM, greet_plane, 0)
    lax.fori_loop(1, NB, greet_column, 0)

    own_down = pltpu.make_async_copy(w_down, down.at[:, pl.ds(0, HID), :], lsem)
    own_down.start()

    row = lax.broadcasted_iota(jnp.int32, (EXPERTS, TOK), 0)
    named = [routes[k : k + 1, :] == row for k in range(2)]
    chosen = jnp.logical_or(named[0], named[1]).astype(F32)
    earlier = lax.broadcasted_iota(jnp.int32, (TOK, TOK), 0) < lax.broadcasted_iota(jnp.int32, (TOK, TOK), 1)
    places = dot(chosen.astype(BF), earlier.astype(F32).astype(BF))
    weight = sum(jnp.where(named[k], gates[k : k + 1, :], 0.0) for k in range(2))
    own_place = jnp.sum(jnp.where(row == branch // 2, jnp.where(chosen > 0, places, -4.0), 0.0), axis=0, keepdims=True)
    spot = lax.broadcasted_iota(jnp.int32, (PAD, TOK), 0)
    wanted = jnp.where(spot < SLOTS, core * SLOTS + spot, -2).astype(F32)
    pick = (wanted == own_place).astype(F32).astype(BF)

    for g in range(NM):
        cols = slice(g * COLS, (g + 1) * COLS)
        cot_send[g] = dot(pick, cots[:, cols]).astype(BF)
    for g in range(NM):
        cols = slice(g * COLS, (g + 1) * COLS)
        x_all[me, :, cols] = dot(pick, tokens[:, cols]).astype(BF)
    cot_all[me] = cot_send[me]

    pl.semaphore_wait(barrier, NM - 1 + NB - 1)

    cot_copies = []
    for d in range(1, NM):
        to = (me + d) % NM
        cot_copies.append(net.send(cot_send.at[to], cot_all.at[me], (branch, to)))

    def gather_start(buf):
        return {
            "a": [net.send(buf.at[me], buf.at[me], in_plane(1, 0)), net.send(buf.at[me], buf.at[me], in_plane(-1, 0))],
            "b": [[net.send(buf.at[me], buf.at[me], in_plane(0, 1)), net.send(buf.at[me], buf.at[me], in_plane(0, -1))]],
        }

    def gather_a1(buf, st, half):
        st["h"] = []
        for i, da in ((0, -1), (1, 1)):
            st["a"][i].wait_recv()
            blk = buf.at[at(da, 0)]
            st["h"].append(net.send(half(blk, i), half(blk, i), in_plane(-da, 0)))
        for da in (-1, 1):
            blk = buf.at[at(da, 0)]
            st["b"].append([net.send(blk, blk, in_plane(0, 1)), net.send(blk, blk, in_plane(0, -1))])
        st["g"] = []

    def gather_a2(buf, st):
        for h in st["h"]:
            h.wait_recv()
        blk = buf.at[at(2, 0)]
        st["b"].append([net.send(blk, blk, in_plane(0, 1)), net.send(blk, blk, in_plane(0, -1))])

    def gather_b1(buf, st, half, n):
        da = (0, -1, 1, 2)[n]
        pair = []
        for i, db in ((0, -1), (1, 1)):
            st["b"][n][i].wait_recv()
            part = half(buf.at[at(da, db)], i ^ (n & 1))
            pair.append(net.send(part, part, in_plane(0, -db)))
        st["g"].append(pair)

    def gather_b2(st, n):
        for g in st["g"][n]:
            g.wait_recv()

    ORDER = (2, 1, -1, 0)

    def reduce_a1(buf, opp, half, st):
        st["o"], st["n"], st["m"], st["bm"] = [], [], [], []
        for j, db in enumerate(ORDER):
            blk, f = buf.at[at(2, db)], j & 1
            st["o"].append([net.send(half(blk, f), half(opp.at[0, j], f), in_plane(1, 0)),
                            net.send(half(blk, 1 - f), half(opp.at[1, j], 1 - f), in_plane(-1, 0))])

    def reduce_a2(buf, acc_in, half, st, js=range(4)):
        for j in js:
            db, f = ORDER[j], j & 1
            up, dn = buf.at[at(1, db)], buf.at[at(-1, db)]
            st["n"].append([net.send(half(up, 1 - f), half(acc_in.at[0, j], 1 - f), in_plane(1, 0)),
                            net.send(half(dn, f), half(acc_in.at[1, j], f), in_plane(-1, 0))])

    def add_to(dst, src):
        dst[...] = (dst[...].astype(F32) + src[...].astype(F32)).astype(BF)

    def reduce_a3(buf, opp, acc_in, half, st, j):
        db, f = ORDER[j], j & 1
        pair = []
        for i, da in ((0, 1), (1, -1)):
            st["o"][j][i].wait_recv()
            blk = half(buf.at[at(da, db)], i ^ f)
            add_to(blk, half(opp.at[i, j], i ^ f))
            pair.append(net.send(blk, half(acc_in.at[i, j], i ^ f), in_plane(da, 0)))
        st["m"].append(pair)

    def reduce_a4(buf, acc_in, whole, st, j):
        db = ORDER[j]
        for i in (0, 1):
            st["n"][j][i].wait_recv()
            st["m"][j][i].wait_recv()
        blk, left, right = whole(buf.at[at(0, db)]), whole(acc_in.at[0, j]), whole(acc_in.at[1, j])
        blk[...] = (blk[...].astype(F32) + left[...].astype(F32) + right[...].astype(F32)).astype(BF)

    def reduce_b1(buf, opp, half, st):
        blk = buf.at[at(0, 2)]
        st["bo"] = [net.send(half(blk, 0), half(opp.at[0], 0), in_plane(0, 1)),
                    net.send(half(blk, 1), half(opp.at[1], 1), in_plane(0, -1))]

    def reduce_b2(buf, acc_in, half, st):
        up, dn = buf.at[at(0, 1)], buf.at[at(0, -1)]
        st["bn"] = [net.send(half(up, 1), half(acc_in.at[0], 1), in_plane(0, 1)),
                    net.send(half(dn, 0), half(acc_in.at[1], 0), in_plane(0, -1))]

    def reduce_b3(buf, opp, acc_in, half, st):
        for i, db in ((0, 1), (1, -1)):
            st["bo"][i].wait_recv()
            blk = half(buf.at[at(0, db)], i)
            add_to(blk, half(opp.at[i], i))
            st["bm"].append(net.send(blk, half(acc_in.at[i], i), in_plane(0, db)))

    def reduce_b4(st):
        for i in (0, 1):
            st["bn"][i].wait_recv()
            st["bm"][i].wait_recv()

    toks = gather_start(x_all)
    DAS = (2, 1, -1, 0)
    down_part = {}
    for da in DAS:
        down_part[da] = []
        for j in range(4):
            m = at(j, da)
            down_part[da].append(net.send(w_down.at[m], down.at[m, pl.ds(HID, HID), :], partner))

    comb[...] = jnp.zeros_like(comb)
    spot = lax.broadcasted_iota(jnp.int32, (2 * PAD, TOK), 0)
    slot = jnp.where(spot % PAD < SLOTS, spot // PAD * SLOTS + spot % PAD, -2).astype(F32)
    for e in range(EXPERTS):
        rows = slice(2 * PAD * e, 2 * PAD * (e + 1))
        comb[rows, 0:TOK] = jnp.where(slot == places[e : e + 1, :], weight[e : e + 1, :], 0.0)

    for c in cot_copies:
        c.wait_recv()
    cot_rows = dot(to_slot_major(), cot_all[...].reshape(PROWS, COLS)).astype(BF)
    own_down.wait()

    def partials(da):
        for c in down_part[da]:
            c.wait_recv()

        def one(j, _):
            m = at(da, j)
            bp[m] = dot_nt(cot_rows, down[m]).astype(BF)
            return 0

        lax.fori_loop(0, 4, one, 0)

    rs = {}
    partials(2)
    reduce_a1(bp, ra_opp, row_half, rs)
    gather_a1(x_all, toks, lane_half)
    partials(1)
    partials(-1)
    in_part = []
    for i in range(NK):
        cols = pl.ds(i * KC, KC)
        in_part.append([net.send(w_in.at[g, :, cols], w_part.at[g, :, cols], partner) for g in range(2)])
    gather_b1(x_all, toks, lane_half, 0)
    gather_a2(x_all, toks)
    partials(0)
    gather_b1(x_all, toks, lane_half, 1)
    reduce_a2(bp, ra, row_half, rs, (0, 1))
    gather_b1(x_all, toks, lane_half, 2)
    gather_b1(x_all, toks, lane_half, 3)
    reduce_a2(bp, ra, row_half, rs, (2, 3))
    for j in range(4):
        reduce_a3(bp, ra_opp, ra, row_half, rs, j)
    for n in range(4):
        gather_b2(toks, n)
    for c in sum(in_part, []):
        c.wait_recv()

    def tiles(i, slot):
        cols = pl.ds(pl.multiple_of(i * KC, KC), KC)
        return [
            pltpu.make_async_copy(src.at[g, :, cols], wbuf.at[slot, g, pl.ds(o * HID, HID), :], wsem.at[slot, g, o])
            for o, src in enumerate((w_in, w_part))
            for g in range(2)
        ]

    def prime():
        for i in range(WB - 1):
            for c in tiles(i, i):
                c.start()

    def stream(lo, hi, body):
        def one(i, _):
            @pl.when(i + WB - 1 < NK)
            def _():
                for c in tiles(i + WB - 1, (i + WB - 1) % WB):
                    c.start()

            slot = i % WB
            for c in tiles(i, slot):
                c.wait()
            body(i, slot)
            return 0

        lax.fori_loop(lo, hi, one, 0)

    pgate[...] = jnp.zeros_like(pgate)
    pup[...] = jnp.zeros_like(pup)

    def forward(i, slot):
        cols = pl.ds(pl.multiple_of(i * KC, KC), KC)
        rows = dot(to_slot_major(), x_all[:, :, cols].reshape(PROWS, KC)).astype(BF)
        pgate[...] += dot_nt(rows, wbuf[slot, 0])
        pup[...] += dot_nt(rows, wbuf[slot, 1])

    prime()
    stream(0, 5, forward)
    reduce_a4(bp, ra, whole, rs, 0)
    reduce_b1(bp, rb_opp, row_half, rs)
    stream(5, NK, forward)

    def activate(i, _):
        r = pl.ds(pl.multiple_of(i * 16, 16), 16)
        g = pgate[r, :]
        s = 1.0 / (1.0 + jnp.exp(-g))
        act_all[me, r, :] = (g * s * pup[r, :]).astype(BF)
        return 0

    lax.fori_loop(0, SLOTS, activate, 0)
    acts = gather_start(act_all)

    reduce_a4(bp, ra, whole, rs, 1)
    reduce_a4(bp, ra, whole, rs, 2)
    reduce_b2(bp, rb, row_half, rs)
    reduce_b3(bp, rb_opp, rb, row_half, rs)
    reduce_a4(bp, ra, whole, rs, 3)
    gather_a1(act_all, acts, row_half)
    reduce_b4(rs)

    def gradients(i, _):
        r = pl.ds(pl.multiple_of(i * 16, 16), 16)
        h = bp[me, r, :].astype(F32) + rb[0, r, :].astype(F32) + rb[1, r, :].astype(F32)
        g, u = pgate[r, :], pup[r, :]
        s = 1.0 / (1.0 + jnp.exp(-g))
        pgate[r, :] = h * u * s * (1.0 + g * (1.0 - s))
        pup[r, :] = h * g * s
        return 0

    lax.fori_loop(0, SLOTS, gradients, 0)
    for w, src in enumerate((pgate, pup)):
        grads[w] = dot(to_token_major(), src[...].astype(BF)).astype(BF)

    for c in toks["a"] + toks["h"] + sum(toks["b"], []) + sum(toks["g"], []):
        c.wait_send()

    def backward(i, slot):
        cols = pl.ds(pl.multiple_of(i * KC, KC), KC)
        total = dot(grads[0], wbuf[slot, 0]) + dot(grads[1], wbuf[slot, 1])
        x_all[:, :, cols] = total.astype(BF).reshape(NM, PAD, KC)

    def quarter(q):
        return lambda ref, h: ref.at[:, pl.ds(q * (D // 2) + h * (D // 4), D // 4)]

    def half_of(q):
        return lambda ref: ref.at[:, pl.ds(q * (D // 2), D // 2)]

    ri_st = [{}, {}]

    def launch(q):
        reduce_a1(x_all, ri_opp, quarter(q), ri_st[q])
        reduce_a2(x_all, ri, quarter(q), ri_st[q])

    prime()
    stream(0, 2, backward)
    gather_a2(act_all, acts)
    gather_b1(act_all, acts, row_half, 0)
    stream(2, 4, backward)
    launch(0)
    gather_b1(act_all, acts, row_half, 1)
    stream(4, 6, backward)
    gather_b1(act_all, acts, row_half, 2)
    stream(6, NK, backward)
    launch(1)
    gather_b1(act_all, acts, row_half, 3)

    def outs(da, db):
        m = at(da, db)
        return dot(act_all[m], down[m])

    out_acc[...] = outs(0, 0)
    for da, db in ((-1, 0), (1, 0), (2, 0)):
        out_acc[...] += outs(da, db)
    for j in range(4):
        reduce_a3(x_all, ri_opp, ri, quarter(0), ri_st[0], j)
    for da in (0, -1, 1, 2):
        for db in (-1, 1):
            out_acc[...] += outs(da, db)
    for j in range(4):
        reduce_a3(x_all, ri_opp, ri, quarter(1), ri_st[1], j)
    for j in range(4):
        reduce_a4(x_all, ri, half_of(0), ri_st[0], j)
        if j == 0:
            reduce_b1(x_all, rj_opp, quarter(0), ri_st[0])
        if j == 2:
            reduce_b2(x_all, rj, quarter(0), ri_st[0])
    for n, da in enumerate((0, -1, 1, 2)):
        gather_b2(acts, n)
        out_acc[...] += outs(da, 2)
    o_send[...] = dot(to_token_major(), out_acc[...].astype(BF)).astype(BF).reshape(NM, PAD, COLS)
    o_all[me] = o_send[me]
    o_copies = []
    for d in range(1, NM):
        to = (me + d) % NM
        o_copies.append(net.send(o_send.at[to], o_all.at[me], (branch, to)))
    for j in range(4):
        reduce_a4(x_all, ri, half_of(1), ri_st[1], j)
        if j == 0:
            reduce_b1(x_all, rj_opp, quarter(1), ri_st[1])
        if j == 2:
            reduce_b2(x_all, rj, quarter(1), ri_st[1])
    for q in range(2):
        reduce_b3(x_all, rj_opp, rj, quarter(q), ri_st[q])
    for c in o_copies:
        c.wait_recv()
    out_in[branch] = o_all[pl.ds(2 * branch, 2)]
    finals = []
    for d in range(1, NB):
        to = (branch + d) % NB
        finals.append(net.send(o_all.at[pl.ds(2 * to, 2)], out_in.at[branch], (to, me)))
    for g in range(NB):
        if g % 4 == 0:
            reduce_b4(ri_st[g // 4])
        cols = slice(g * OUTC, (g + 1) * OUTC)
        y_send[g] = (
            x_all[me, :, cols].astype(F32) + rj[0, :, cols].astype(F32) + rj[1, :, cols].astype(F32)
        ).astype(BF)
    back_in[branch] = y_send[branch]
    for d in range(1, NB):
        to = (branch + d) % NB
        finals.append(net.send(y_send.at[to], back_in.at[branch], (to, me)))

    weights = comb[...].T[0:TOK, :]
    hi = weights.astype(BF)
    lo = (weights - hi.astype(F32)).astype(BF)
    for c in finals[: NB - 1]:
        c.wait_recv()
    for j in range(2):
        got = out_in[:, j].reshape(NB * PAD, COLS)
        out_ref[:, j * COLS : (j + 1) * COLS] = (dot(hi, got) + dot(lo, got)).astype(BF)
    for c in finals[NB - 1 :]:
        c.wait_recv()
    got = back_in[...].reshape(NB * PAD, OUTC)
    back_ref[...] = (dot(hi, got) + dot(lo, got)).astype(BF)

    reused = toks["a"] + toks["h"] + sum(toks["b"], []) + sum(toks["g"], [])
    for c in net.started:
        if not any(c is r for r in reused):
            c.wait_send()


N_COPIES = 240


def on_device(tokens, cotangent, routes, router_gates, expert_in, expert_down):
    vm = pl.BlockSpec(memory_space=pltpu.VMEM)
    hbm = pl.BlockSpec(memory_space=pl.ANY)
    out, back, _ = pl.pallas_call(
        kernel,
        out_shape=(
            jax.ShapeDtypeStruct((TOK, OUTC), BF),
            jax.ShapeDtypeStruct((TOK, OUTC), BF),
            jax.ShapeDtypeStruct((2, HID, D), BF),
        ),
        in_specs=[vm, vm, vm, vm, hbm, hbm],
        out_specs=(vm, vm, hbm),
        scratch_shapes=[
            pltpu.VMEM((NM, PAD, D), BF),
            pltpu.VMEM((NM, PAD, COLS), BF),
            pltpu.VMEM((NM, PAD, COLS), BF),
            pltpu.VMEM((NM, CH, COLS), BF),
            pltpu.VMEM((NM, ROWS, CH), BF),
            pltpu.VMEM((2, 4, ROWS, CH), BF),
            pltpu.VMEM((2, 4, ROWS, CH), BF),
            pltpu.VMEM((2, ROWS, CH), BF),
            pltpu.VMEM((2, ROWS, CH), BF),
            pltpu.VMEM((NM, ROWS, CH), BF),
            pltpu.VMEM((WB, 2, CH, KC), BF),
            pltpu.VMEM((ROWS, CH), F32),
            pltpu.VMEM((ROWS, CH), F32),
            pltpu.VMEM((2, PROWS, CH), BF),
            pltpu.VMEM((2, 4, PAD, D), BF),
            pltpu.VMEM((2, 4, PAD, D), BF),
            pltpu.VMEM((2, PAD, D), BF),
            pltpu.VMEM((2, PAD, D), BF),
            pltpu.VMEM((ROWS, COLS), F32),
            pltpu.VMEM((NM, PAD, COLS), BF),
            pltpu.VMEM((NM, PAD, COLS), BF),
            pltpu.VMEM((NB, 2, PAD, COLS), BF),
            pltpu.VMEM((NB, PAD, OUTC), BF),
            pltpu.VMEM((NB, PAD, OUTC), BF),
            pltpu.VMEM((NB * PAD, 128), F32),
            pltpu.SemaphoreType.DMA((N_COPIES,)),
            pltpu.SemaphoreType.DMA((N_COPIES,)),
            pltpu.SemaphoreType.DMA,
            pltpu.SemaphoreType.DMA((WB, 2, 2)),
        ],
        compiler_params=pltpu.CompilerParams(
            collective_id=0, has_side_effects=True, vmem_limit_bytes=66060288
        ),
        name="expert_step",
    )(tokens, cotangent, routes.T, router_gates.T, expert_in.transpose(0, 2, 1), expert_down.reshape(NM, HID, COLS))
    return out, back


def solution(mesh):
    placed = (
        P("mp", None),
        P("mp", None),
        P("mp", None),
        P("mp", None),
        P(None, None, ("branch", "mp")),
        P("branch", "mp"),
    )
    return jax.shard_map(
        on_device,
        mesh=mesh,
        in_specs=placed,
        out_specs=(P("mp", "branch"), P("mp", "branch")),
        check_vma=False,
    )
```

```python
import functools

import jax
import jax.numpy as jnp
from jax import lax
from jax.experimental import pallas as pl
from jax.experimental.pallas import tpu as pltpu
from jax.sharding import PartitionSpec as P

MESH = pl.DeviceIdType.MESH
BF = jnp.bfloat16
F32 = jnp.float32

EXPERTS = 4
NB = 8
NM = 16
TOK = 48
D = 8192
HID = 448
CH = 2 * HID
SLOTS = 15
PAD = 16
ROWS = SLOTS * NM
PROWS = PAD * NM
COLS = D // NM
OUTC = D // NB
KC = 1024
NK = D // KC
WB = 2
HALF0 = 128


def dot(a, b):
    return jnp.dot(a, b, preferred_element_type=F32)


def dot_nt(a, b):
    return lax.dot_general(a, b, (((1,), (1,)), ((), ())), preferred_element_type=F32)


def to_slot_major():
    q = lax.broadcasted_iota(jnp.int32, (ROWS, PROWS), 0)
    r = lax.broadcasted_iota(jnp.int32, (ROWS, PROWS), 1)
    return (r == (q % 16) * 16 + q // 16).astype(F32).astype(BF)


def to_token_major():
    r = lax.broadcasted_iota(jnp.int32, (PROWS, ROWS), 0)
    q = lax.broadcasted_iota(jnp.int32, (PROWS, ROWS), 1)
    return (r == (q % 16) * 16 + q // 16).astype(F32).astype(BF)


def wait_bytes(ref, sem):
    pltpu.make_async_copy(ref, ref, sem).wait()


class Flow:
    def __init__(self, net):
        self.net, self.sem = net, net.send_sem.at[net.flows]
        net.flows += 1


class Net:
    def __init__(self, send_sem, recv_sem):
        self.send_sem, self.recv_sem = send_sem, recv_sem
        self.flows = self.groups = 0

    def group(self):
        self.groups += 1
        return self.recv_sem.at[self.groups - 1]

    def send(self, flow, group, src, dst, device):
        pltpu.make_async_remote_copy(
            src_ref=src,
            dst_ref=dst,
            send_sem=flow.sem,
            recv_sem=group,
            device_id=device,
            device_id_type=MESH,
        ).start()


def row_half(ref, h):
    return ref.at[pl.ds(0, HALF0), :] if h == 0 else ref.at[pl.ds(HALF0, ROWS - HALF0), :]


def whole(ref):
    return ref


def lane_half(ref, h):
    return ref.at[:, pl.ds(h * (D // 2), D // 2)]


def kernel(
    tokens_hbm, cots_hbm, routes, gates, w_in, w_down,
    out_ref, back_ref, w_part,
    x_all, cot_send, cot_all, down, bp, ra_opp, ra, rb_opp, rb,
    act_all, wbuf, pgate, pup, grads, ri_opp, ri, rj_opp, rj,
    out_acc, o_send, o_all, out_in, y_send, back_in, comb, tokens, cots,
    send_sem, recv_sem, lsem, wsem,
):
    branch = lax.axis_index("branch")
    me = lax.axis_index("mp")
    core = branch % 2
    s_a, s_b = 1 + 3 * core, 4 - 3 * core
    a0, b0 = (me // s_a) % 4, (me // s_b) % 4

    def at(da, db):
        return ((a0 + da + 4) % 4) * s_a + ((b0 + db + 4) % 4) * s_b

    def in_plane(da, db):
        return (branch, at(da, db))

    partner = (branch + 1 - 2 * core, me)
    net = Net(send_sem, recv_sem)

    barrier = pltpu.get_barrier_semaphore()

    def greet_plane(d, _):
        pl.semaphore_signal(barrier, inc=1, device_id=(branch, (me + d) % NM), device_id_type=MESH)
        return 0

    def greet_column(d, _):
        pl.semaphore_signal(barrier, inc=1, device_id=((branch + d) % NB, me), device_id_type=MESH)
        return 0

    lax.fori_loop(1, NM, greet_plane, 0)
    lax.fori_loop(1, NB, greet_column, 0)

    loads = [
        pltpu.make_async_copy(src, dst, lsem.at[i])
        for i, (src, dst) in enumerate(((cots_hbm, cots), (tokens_hbm, tokens)))
    ]
    for c in loads:
        c.start()

    own_down = pltpu.make_async_copy(w_down, down.at[:, pl.ds(0, HID), :], lsem.at[2])
    own_down.start()

    row = lax.broadcasted_iota(jnp.int32, (EXPERTS, TOK), 0)
    named = [routes[k : k + 1, :] == row for k in range(2)]
    chosen = jnp.logical_or(named[0], named[1]).astype(F32)
    earlier = lax.broadcasted_iota(jnp.int32, (TOK, TOK), 0) < lax.broadcasted_iota(jnp.int32, (TOK, TOK), 1)
    places = dot(chosen.astype(BF), earlier.astype(F32).astype(BF))
    weight = sum(jnp.where(named[k], gates[k : k + 1, :], 0.0) for k in range(2))
    own_place = jnp.sum(jnp.where(row == branch // 2, jnp.where(chosen > 0, places, -4.0), 0.0), axis=0, keepdims=True)
    spot = lax.broadcasted_iota(jnp.int32, (PAD, TOK), 0)
    wanted = jnp.where(spot < SLOTS, core * SLOTS + spot, -2).astype(F32)
    pick = (wanted == own_place).astype(F32).astype(BF)

    loads[0].wait()
    for g in range(NM):
        cols = slice(g * COLS, (g + 1) * COLS)
        cot_send[g] = dot(pick, cots[:, cols]).astype(BF)
    loads[1].wait()
    for g in range(NM):
        cols = slice(g * COLS, (g + 1) * COLS)
        x_all[me, :, cols] = dot(pick, tokens[:, cols]).astype(BF)
    cot_all[me] = cot_send[me]

    pl.semaphore_wait(barrier, NM - 1 + NB - 1)

    cot_flow, cot_group = Flow(net), net.group()
    for d in range(1, NM):
        to = (me + d) % NM
        net.send(cot_flow, cot_group, cot_send.at[to], cot_all.at[me], (branch, to))

    def both_b(buf, st, da):
        blk, g = buf.at[at(da, 0)], net.group()
        for db in (1, -1):
            net.send(st["flow"], g, blk, blk, in_plane(0, db))
        st["b"].append(g)

    def gather_start(buf):
        st = {"flow": Flow(net), "a": net.group(), "b": [], "g": []}
        for da in (1, -1):
            net.send(st["flow"], st["a"], buf.at[me], buf.at[me], in_plane(da, 0))
        both_b(buf, st, 0)
        return st

    def gather_a1(buf, st, half):
        wait_bytes(buf.at[pl.ds(0, 2)], st["a"])
        st["h"] = net.group()
        for i, da in ((0, -1), (1, 1)):
            part = half(buf.at[at(da, 0)], i)
            net.send(st["flow"], st["h"], part, part, in_plane(-da, 0))
        both_b(buf, st, -1)
        both_b(buf, st, 1)

    def gather_a2(buf, st):
        wait_bytes(buf.at[0], st["h"])
        both_b(buf, st, 2)

    def gather_b1(buf, st, half, n):
        da = (0, -1, 1, 2)[n]
        wait_bytes(buf.at[pl.ds(0, 2)], st["b"][n])
        g = net.group()
        for i, db in ((0, -1), (1, 1)):
            part = half(buf.at[at(da, db)], i ^ (n & 1))
            net.send(st["flow"], g, part, part, in_plane(0, -db))
        st["g"].append(g)

    def gather_b2(buf, st, n):
        wait_bytes(buf.at[0], st["g"][n])

    def sent(buf, st):
        wait_bytes(buf.at[pl.ds(0, NM - 1)], st["flow"].sem)

    ORDER = (2, 1, -1, 0)

    def reduce_a1(buf, opp, half, st):
        st["o"], st["n"] = [], [net.group() for _ in ORDER]
        st["bo"], st["bn"] = net.group(), net.group()
        for j, db in enumerate(ORDER):
            blk, f, g = buf.at[at(2, db)], j & 1, net.group()
            net.send(st["flow"], g, half(blk, f), half(opp.at[0, j], f), in_plane(1, 0))
            net.send(st["flow"], g, half(blk, 1 - f), half(opp.at[1, j], 1 - f), in_plane(-1, 0))
            st["o"].append(g)

    def reduce_a2(buf, acc_in, half, st, js=range(4)):
        for j in js:
            db, f, g = ORDER[j], j & 1, st["n"][j]
            up, dn = buf.at[at(1, db)], buf.at[at(-1, db)]
            net.send(st["flow"], g, half(up, 1 - f), half(acc_in.at[0, j], 1 - f), in_plane(1, 0))
            net.send(st["flow"], g, half(dn, f), half(acc_in.at[1, j], f), in_plane(-1, 0))

    def add_to(dst, src):
        dst[...] = (dst[...].astype(F32) + src[...].astype(F32)).astype(BF)

    def reduce_a3(buf, opp, acc_in, half, whole, st, j):
        db, f = ORDER[j], j & 1
        wait_bytes(whole(buf.at[0]), st["o"][j])
        for i, da in ((0, 1), (1, -1)):
            blk = half(buf.at[at(da, db)], i ^ f)
            add_to(blk, half(opp.at[i, j], i ^ f))
            net.send(st["flow"], st["n"][j], blk, half(acc_in.at[i, j], i ^ f), in_plane(da, 0))

    def reduce_a4(buf, acc_in, whole, st, j):
        db = ORDER[j]
        wait_bytes(whole(acc_in.at[:, j]), st["n"][j])
        blk, left, right = whole(buf.at[at(0, db)]), whole(acc_in.at[0, j]), whole(acc_in.at[1, j])
        blk[...] = (blk[...].astype(F32) + left[...].astype(F32) + right[...].astype(F32)).astype(BF)

    def reduce_b1(buf, opp, half, st):
        blk = buf.at[at(0, 2)]
        net.send(st["flow"], st["bo"], half(blk, 0), half(opp.at[0], 0), in_plane(0, 1))
        net.send(st["flow"], st["bo"], half(blk, 1), half(opp.at[1], 1), in_plane(0, -1))

    def reduce_b2(buf, acc_in, half, st):
        up, dn = buf.at[at(0, 1)], buf.at[at(0, -1)]
        net.send(st["flow"], st["bn"], half(up, 1), half(acc_in.at[0], 1), in_plane(0, 1))
        net.send(st["flow"], st["bn"], half(dn, 0), half(acc_in.at[1], 0), in_plane(0, -1))

    def reduce_b3(buf, opp, acc_in, half, whole, st):
        wait_bytes(whole(buf.at[0]), st["bo"])
        for i, db in ((0, 1), (1, -1)):
            blk = half(buf.at[at(0, db)], i)
            add_to(blk, half(opp.at[i], i))
            net.send(st["flow"], st["bn"], blk, half(acc_in.at[i], i), in_plane(0, db))

    def reduce_b4(acc_in, whole, st):
        wait_bytes(whole(acc_in), st["bn"])

    toks = gather_start(x_all)
    DAS = (2, 1, -1, 0)
    down_flow, down_part = Flow(net), {}
    for da in DAS:
        down_part[da] = net.group()
        for j in range(4):
            m = at(j, da)
            net.send(down_flow, down_part[da], w_down.at[m], down.at[m, pl.ds(HID, HID), :], partner)

    comb[...] = jnp.zeros_like(comb)
    spot = lax.broadcasted_iota(jnp.int32, (2 * PAD, TOK), 0)
    slot = jnp.where(spot % PAD < SLOTS, spot // PAD * SLOTS + spot % PAD, -2).astype(F32)
    for e in range(EXPERTS):
        rows = slice(2 * PAD * e, 2 * PAD * (e + 1))
        comb[rows, 0:TOK] = jnp.where(slot == places[e : e + 1, :], weight[e : e + 1, :], 0.0)

    wait_bytes(cot_all.at[pl.ds(0, NM - 1)], cot_group)
    cot_rows = dot(to_slot_major(), cot_all[...].reshape(PROWS, COLS)).astype(BF)
    own_down.wait()

    def partials(da):
        wait_bytes(w_down.at[pl.ds(0, 4)], down_part[da])

        def one(j, _):
            m = at(da, j)
            bp[m] = dot_nt(cot_rows, down[m]).astype(BF)
            return 0

        lax.fori_loop(0, 4, one, 0)

    rs = {"flow": Flow(net)}
    partials(2)
    reduce_a1(bp, ra_opp, row_half, rs)
    gather_a1(x_all, toks, lane_half)
    partials(1)
    partials(-1)
    in_flow, in_group = Flow(net), net.group()
    net.send(in_flow, in_group, w_in, w_part, partner)
    gather_b1(x_all, toks, lane_half, 0)
    gather_a2(x_all, toks)
    partials(0)
    gather_b1(x_all, toks, lane_half, 1)
    reduce_a2(bp, ra, row_half, rs, (0, 1))
    gather_b1(x_all, toks, lane_half, 2)
    gather_b1(x_all, toks, lane_half, 3)
    reduce_a2(bp, ra, row_half, rs, (2, 3))
    for j in range(4):
        reduce_a3(bp, ra_opp, ra, row_half, whole, rs, j)
    for n in range(4):
        gather_b2(x_all, toks, n)
    wait_bytes(w_part, in_group)

    def tiles(i, slot):
        cols = pl.ds(pl.multiple_of(i * KC, KC), KC)
        return [
            pltpu.make_async_copy(src.at[g, :, cols], wbuf.at[slot, g, pl.ds(o * HID, HID), :], wsem.at[slot, g, o])
            for o, src in enumerate((w_in, w_part))
            for g in range(2)
        ]

    def prime():
        for i in range(WB - 1):
            for c in tiles(i, i):
                c.start()

    def stream(lo, hi, body):
        def one(i, _):
            @pl.when(i + WB - 1 < NK)
            def _():
                for c in tiles(i + WB - 1, (i + WB - 1) % WB):
                    c.start()

            slot = i % WB
            for c in tiles(i, slot):
                c.wait()
            body(i, slot)
            return 0

        lax.fori_loop(lo, hi, one, 0)

    pgate[...] = jnp.zeros_like(pgate)
    pup[...] = jnp.zeros_like(pup)

    def forward(i, slot):
        cols = pl.ds(pl.multiple_of(i * KC, KC), KC)
        rows = dot(to_slot_major(), x_all[:, :, cols].reshape(PROWS, KC)).astype(BF)
        pgate[...] += dot_nt(rows, wbuf[slot, 0])
        pup[...] += dot_nt(rows, wbuf[slot, 1])

    prime()
    stream(0, 5, forward)
    reduce_a4(bp, ra, whole, rs, 0)
    reduce_b1(bp, rb_opp, row_half, rs)
    stream(5, NK, forward)

    def activate(i, _):
        r = pl.ds(pl.multiple_of(i * 16, 16), 16)
        g = pgate[r, :]
        s = 1.0 / (1.0 + jnp.exp(-g))
        act_all[me, r, :] = (g * s * pup[r, :]).astype(BF)
        return 0

    lax.fori_loop(0, SLOTS, activate, 0)
    acts = gather_start(act_all)

    reduce_a4(bp, ra, whole, rs, 1)
    reduce_a4(bp, ra, whole, rs, 2)
    reduce_b2(bp, rb, row_half, rs)
    reduce_b3(bp, rb_opp, rb, row_half, whole, rs)
    reduce_a4(bp, ra, whole, rs, 3)
    gather_a1(act_all, acts, row_half)
    reduce_b4(rb, whole, rs)

    def gradients(i, _):
        r = pl.ds(pl.multiple_of(i * 16, 16), 16)
        h = bp[me, r, :].astype(F32) + rb[0, r, :].astype(F32) + rb[1, r, :].astype(F32)
        g, u = pgate[r, :], pup[r, :]
        s = 1.0 / (1.0 + jnp.exp(-g))
        pgate[r, :] = h * u * s * (1.0 + g * (1.0 - s))
        pup[r, :] = h * g * s
        return 0

    lax.fori_loop(0, SLOTS, gradients, 0)
    for w, src in enumerate((pgate, pup)):
        grads[w] = dot(to_token_major(), src[...].astype(BF)).astype(BF)

    sent(x_all, toks)

    def backward(i, slot):
        cols = pl.ds(pl.multiple_of(i * KC, KC), KC)
        total = dot(grads[0], wbuf[slot, 0]) + dot(grads[1], wbuf[slot, 1])
        x_all[:, :, cols] = total.astype(BF).reshape(NM, PAD, KC)

    def quarter(q):
        return lambda ref, h: ref.at[:, pl.ds(q * (D // 2) + h * (D // 4), D // 4)]

    def half_of(q):
        return lambda ref: ref.at[..., pl.ds(q * (D // 2), D // 2)]

    ri_flow = Flow(net)
    ri_st = [{"flow": ri_flow}, {"flow": ri_flow}]

    def launch(q):
        reduce_a1(x_all, ri_opp, quarter(q), ri_st[q])
        reduce_a2(x_all, ri, quarter(q), ri_st[q])

    prime()
    stream(0, 2, backward)
    gather_a2(act_all, acts)
    gather_b1(act_all, acts, row_half, 0)
    stream(2, 4, backward)
    launch(0)
    gather_b1(act_all, acts, row_half, 1)
    stream(4, 6, backward)
    gather_b1(act_all, acts, row_half, 2)
    stream(6, NK, backward)
    launch(1)
    gather_b1(act_all, acts, row_half, 3)

    def outs(da, db):
        m = at(da, db)
        return dot(act_all[m], down[m])

    out_acc[...] = outs(0, 0)
    for da, db in ((-1, 0), (1, 0), (2, 0)):
        out_acc[...] += outs(da, db)
    for j in range(4):
        reduce_a3(x_all, ri_opp, ri, quarter(0), half_of(0), ri_st[0], j)
    for da in (0, -1, 1, 2):
        for db in (-1, 1):
            out_acc[...] += outs(da, db)
    for j in range(4):
        reduce_a3(x_all, ri_opp, ri, quarter(1), half_of(1), ri_st[1], j)
    for j in range(4):
        reduce_a4(x_all, ri, half_of(0), ri_st[0], j)
        if j == 0:
            reduce_b1(x_all, rj_opp, quarter(0), ri_st[0])
        if j == 2:
            reduce_b2(x_all, rj, quarter(0), ri_st[0])
    for n, da in enumerate((0, -1, 1, 2)):
        gather_b2(act_all, acts, n)
        out_acc[...] += outs(da, 2)
    o_send[...] = dot(to_token_major(), out_acc[...].astype(BF)).astype(BF).reshape(NM, PAD, COLS)
    o_all[me] = o_send[me]
    o_flow, o_group = Flow(net), net.group()
    for d in range(1, NM):
        to = (me + d) % NM
        net.send(o_flow, o_group, o_send.at[to], o_all.at[me], (branch, to))
    for j in range(4):
        reduce_a4(x_all, ri, half_of(1), ri_st[1], j)
        if j == 0:
            reduce_b1(x_all, rj_opp, quarter(1), ri_st[1])
        if j == 2:
            reduce_b2(x_all, rj, quarter(1), ri_st[1])
    for q in range(2):
        reduce_b3(x_all, rj_opp, rj, quarter(q), half_of(q), ri_st[q])
    wait_bytes(o_all.at[pl.ds(0, NM - 1)], o_group)
    out_in[branch] = o_all[pl.ds(2 * branch, 2)]
    out_flow, out_group = Flow(net), net.group()
    for d in range(1, NB):
        to = (branch + d) % NB
        net.send(out_flow, out_group, o_all.at[pl.ds(2 * to, 2)], out_in.at[branch], (to, me))
    for g in range(NB):
        if g % 4 == 0:
            reduce_b4(rj, half_of(g // 4), ri_st[g // 4])
        cols = slice(g * OUTC, (g + 1) * OUTC)
        y_send[g] = (
            x_all[me, :, cols].astype(F32) + rj[0, :, cols].astype(F32) + rj[1, :, cols].astype(F32)
        ).astype(BF)
    back_in[branch] = y_send[branch]
    back_flow, back_group = Flow(net), net.group()
    for d in range(1, NB):
        to = (branch + d) % NB
        net.send(back_flow, back_group, y_send.at[to], back_in.at[branch], (to, me))

    weights = comb[...].T[0:TOK, :]
    hi = weights.astype(BF)
    lo = (weights - hi.astype(F32)).astype(BF)
    wait_bytes(out_in.at[pl.ds(0, NB - 1)], out_group)
    for j in range(2):
        got = out_in[:, j].reshape(NB * PAD, COLS)
        out_ref[:, j * COLS : (j + 1) * COLS] = (dot(hi, got) + dot(lo, got)).astype(BF)
    wait_bytes(back_in.at[pl.ds(0, NB - 1)], back_group)
    got = back_in[...].reshape(NB * PAD, OUTC)
    back_ref[...] = (dot(hi, got) + dot(lo, got)).astype(BF)

    wait_bytes(cot_send.at[pl.ds(0, NM - 1)], cot_flow.sem)
    wait_bytes(w_down, down_flow.sem)
    wait_bytes(w_in, in_flow.sem)
    sent(bp, rs)
    sent(act_all, acts)
    sent(x_all, ri_st[0])
    wait_bytes(o_send.at[pl.ds(0, NM - 1)], o_flow.sem)
    wait_bytes(out_in.at[pl.ds(0, NB - 1)], out_flow.sem)
    wait_bytes(back_in.at[pl.ds(0, NB - 1)], back_flow.sem)
    assert net.flows == N_FLOWS and net.groups == N_GROUPS, (net.flows, net.groups)


N_FLOWS, N_GROUPS = 10, 59


def on_device(tokens, cotangent, routes, router_gates, expert_in, expert_down):
    vm = pl.BlockSpec(memory_space=pltpu.VMEM)
    hbm = pl.BlockSpec(memory_space=pl.ANY)
    out, back, _ = pl.pallas_call(
        kernel,
        out_shape=(
            jax.ShapeDtypeStruct((TOK, OUTC), BF),
            jax.ShapeDtypeStruct((TOK, OUTC), BF),
            jax.ShapeDtypeStruct((2, HID, D), BF),
        ),
        in_specs=[hbm, hbm, vm, vm, hbm, hbm],
        out_specs=(vm, vm, hbm),
        scratch_shapes=[
            pltpu.VMEM((NM, PAD, D), BF),
            pltpu.VMEM((NM, PAD, COLS), BF),
            pltpu.VMEM((NM, PAD, COLS), BF),
            pltpu.VMEM((NM, CH, COLS), BF),
            pltpu.VMEM((NM, ROWS, CH), BF),
            pltpu.VMEM((2, 4, ROWS, CH), BF),
            pltpu.VMEM((2, 4, ROWS, CH), BF),
            pltpu.VMEM((2, ROWS, CH), BF),
            pltpu.VMEM((2, ROWS, CH), BF),
            pltpu.VMEM((NM, ROWS, CH), BF),
            pltpu.VMEM((WB, 2, CH, KC), BF),
            pltpu.VMEM((ROWS, CH), F32),
            pltpu.VMEM((ROWS, CH), F32),
            pltpu.VMEM((2, PROWS, CH), BF),
            pltpu.VMEM((2, 4, PAD, D), BF),
            pltpu.VMEM((2, 4, PAD, D), BF),
            pltpu.VMEM((2, PAD, D), BF),
            pltpu.VMEM((2, PAD, D), BF),
            pltpu.VMEM((ROWS, COLS), F32),
            pltpu.VMEM((NM, PAD, COLS), BF),
            pltpu.VMEM((NM, PAD, COLS), BF),
            pltpu.VMEM((NB, 2, PAD, COLS), BF),
            pltpu.VMEM((NB, PAD, OUTC), BF),
            pltpu.VMEM((NB, PAD, OUTC), BF),
            pltpu.VMEM((NB * PAD, 128), F32),
            pltpu.VMEM((TOK, D), BF),
            pltpu.VMEM((TOK, D), BF),
            pltpu.SemaphoreType.DMA((N_FLOWS,)),
            pltpu.SemaphoreType.DMA((N_GROUPS,)),
            pltpu.SemaphoreType.DMA((3,)),
            pltpu.SemaphoreType.DMA((WB, 2, 2)),
        ],
        compiler_params=pltpu.CompilerParams(
            collective_id=0, has_side_effects=True, vmem_limit_bytes=66060288
        ),
        name="expert_step",
    )(tokens, cotangent, routes.T, router_gates.T, expert_in.transpose(0, 2, 1), expert_down.reshape(NM, HID, COLS))
    return out, back


def solution(mesh):
    placed = (
        P("mp", None),
        P("mp", None),
        P("mp", None),
        P("mp", None),
        P(None, None, ("branch", "mp")),
        P("branch", "mp"),
    )
    return jax.shard_map(
        on_device,
        mesh=mesh,
        in_specs=placed,
        out_specs=(P("mp", "branch"), P("mp", "branch")),
        check_vma=False,
    )
```
